512 devices in a mesh: tx: 32 (over z, core), ty: 16 (over x, y).
Axes of the slice: x: 4, y: 4, z: 16, core: 2. Of those that a mesh axis runs over, the one named last changes fastest.
Arguments:
- object_planes: float32 [2, 8192, 8192], P(None, 'ty', 'tx'), may hold values from -6 to 6
- probe: float32 [2, 128, 128], replicated, may hold values from -6 to 6
- anchors: int32 [16, 32, 8, 2], P('ty', 'tx'), may hold values from 0 to 8064, as said below
- counts: int32 [16, 32], P('ty', 'tx'), may hold values from 1 to 7, as said below
- intensity: float32 [16, 32, 8, 128, 128], P('ty', 'tx'), may hold values from 0.1 to 3
Outputs:
- object_out: float32 [2, 8192, 8192], P(None, 'ty', 'tx')
- probe_out: float32 [2, 128, 128], replicated
The draws below stay inside these ranges and needn't reach their ends.
Inputs may be any that keep to these rules, and one draw needn't show every extreme that they name: `counts`: each tile holds 1 to 7 live positions; tiles (a, b) and (a, b xor 32 / 2) together hold at most 8; in every draw some such pair holds exactly 8, one of them 8 - 1. `anchors`: every slot's corner lies inside its own tile, and its 128 x 128 patch lies inside the object.
All inputs are finite; a program needn't handle non-finite values.
Results may differ from the reference program's by a relative error of at most 0.0003.
Values sent between devices are 32-bit elements; how exact they have to be, the bound alone decides.
No kernel may reach another device: no remote copies, remote signals or barrier semaphores. Data moves between devices by JAX's collectives and lax.ppermute only.
A program may use at most 64 MiB of HBM per device.

```python
import math
import jax
import jax.numpy as jnp
from jax import lax

W = 128
TR = 512
TC = 256
CAP = 8
ITERS = 2
GRID_R = 16
GRID_C = 32
NR = 8192
NC = 8192
N_TX = 32
N_TY = 16


def draw_counts(key, part):
    key = jax.random.fold_in(key, 11)
    keys = jax.random.split(key, 4)
    half_cols = GRID_C // 2
    total = jax.random.randint(keys[0], (GRID_R, half_cols), CAP // 2, CAP + 1)
    first = jax.random.randint(keys[1], (GRID_R, half_cols), 1, total)
    chosen = jax.random.randint(keys[2], (), 0, GRID_R * half_cols)
    flat = jnp.arange(GRID_R * half_cols).reshape(GRID_R, half_cols)
    total = jnp.where(flat == chosen, CAP, total)
    first = jnp.where(flat == chosen, CAP - 1, first)
    second = total - first
    flip = jax.random.randint(keys[3], (GRID_R, half_cols), 0, 2) == 1
    left = jnp.where(flip, second, first)
    right = jnp.where(flip, first, second)
    return jnp.concatenate([left, right], axis=1).astype(jnp.int32)


def draw_anchors(key, part):
    key = jax.random.fold_in(key, 23)
    keys = jax.random.split(key, 2)
    row_base = (jnp.arange(GRID_R) * TR)[:, None, None]
    row_top = jnp.minimum(TR, NR - W - row_base + 1)
    rows = row_base + jax.random.randint(keys[0], (GRID_R, GRID_C, CAP), 0, row_top)
    col_base = (jnp.arange(GRID_C) * TC)[None, :, None]
    col_top = jnp.minimum(TC, NC - W - col_base + 1)
    cols = col_base + jax.random.randint(keys[1], (GRID_R, GRID_C, CAP), 0, col_top)
    return jnp.stack([rows, cols], axis=-1).astype(jnp.int32)


def levels(stream_key, shape, shards, low, top_value):
    gain = 1.0
    for axis_at, shards_of in shards:
        steps = jax.random.uniform(jax.random.fold_in(jax.random.fold_in(stream_key, 6), axis_at), (shards_of,), jnp.float32, low / len(shards), top_value / len(shards))
        gain = gain * jnp.repeat(jnp.exp(steps), shape[axis_at] // shards_of).reshape((-1,) + (1,) * (len(shape) - 1 - axis_at))
    return gain


def centred(rng, extent, deviation, limit, cuts=(), kind=jnp.bfloat16):
    result = deviation * jax.random.normal(rng, extent, jnp.float32)
    if cuts:
        result = result * levels(rng, extent, cuts, -0.22, 0.18)
    return jnp.clip(result, -limit, limit).astype(kind)


def setup_inputs(seed: int = 0) -> dict:
    key_list = jax.random.split(jax.random.key(seed), 6)
    return {
        "object_planes": centred(key_list[0], (2, NR, NC), 0.7, 6.0, ((1, 16), (2, 32)), jnp.float32),
        "probe": centred(key_list[1], (2, W, W), 0.7, 6.0, (), jnp.float32),
        "anchors": draw_anchors(jax.random.fold_in(key_list[5], 71), 0),
        "counts": draw_counts(jax.random.fold_in(key_list[5], 71), 0),
        "intensity": jnp.clip(jnp.exp(math.log(3.0) - 3.4011974 * jax.random.uniform(key_list[4], (GRID_R, GRID_C, CAP, W, W), jnp.float32) ** levels(key_list[4], (GRID_R, GRID_C, CAP, W, W), ((0, 16), (1, 32)), -0.2, 0.2)), 0.1, 3.0),
    }


step_object = 1.0
step_probe = 1.0


def reference(object_planes, probe, anchors, counts, intensity):
    flat_org = anchors.reshape(-1, 2).astype(jnp.int32)
    live = (jnp.arange(CAP)[None, None, :] < counts[:, :, None]).reshape(-1)
    inten = intensity.reshape(-1, W, W)
    total = flat_org.shape[0]
    planes = object_planes
    current = probe
    for step in range(ITERS):
        wave_probe = current[0] + 1j * current[1]

        def one(index, carry):
            grad, probe_grad = carry
            row = flat_org[index, 0]
            col = flat_org[index, 1]
            patch = lax.dynamic_slice(planes, (jnp.int32(0), row, col), (2, W, W))
            obj = patch[0] + 1j * patch[1]
            far = jnp.fft.fft2(wave_probe * obj, norm="ortho")
            misfit = far.real * far.real + far.imag * far.imag - inten[index]
            back = jnp.fft.ifft2(misfit * far, norm="ortho")
            weight = live[index].astype(planes.dtype)
            obj_term = jnp.conj(wave_probe) * back * weight
            probe_term = jnp.conj(obj) * back * weight
            old = lax.dynamic_slice(grad, (jnp.int32(0), row, col), (2, W, W))
            grad = lax.dynamic_update_slice(grad, old + jnp.stack([obj_term.real, obj_term.imag]), (jnp.int32(0), row, col))
            probe_grad = probe_grad + jnp.stack([probe_term.real, probe_term.imag])
            return grad, probe_grad

        grad, probe_grad = lax.fori_loop(0, total, one, (jnp.zeros_like(planes), jnp.zeros_like(current)))
        peak = jnp.max(current[0] * current[0] + current[1] * current[1]) + 1e-6
        planes = planes - (step_object / peak) * grad
        current = current - (step_probe / (N_TX * N_TY)) * probe_grad
    return planes, current
```

```python
import jax
import jax.numpy as jnp
import numpy as np
from jax import lax
from jax.experimental import pallas as pl
from jax.experimental.pallas import tpu as pltpu
from jax.sharding import PartitionSpec as P

step_object = 1.0
step_probe = 1.0
GROUP = 2
CORES = 2
F32 = jnp.float32
BF16 = jnp.bfloat16


def shift(value, rows, cols):
    n_r, n_c = lax.axis_size("ty"), lax.axis_size("tx")
    if cols == 0:
        return lax.ppermute(
            value, "ty", [(a, a + rows) for a in range(n_r) if 0 <= a + rows < n_r]
        )
    if rows == 0:
        return lax.ppermute(
            value, "tx", [(b, b + cols) for b in range(n_c) if 0 <= b + cols < n_c]
        )
    pairs = [
        (b * n_r + a, (b + cols) * n_r + a + rows)
        for a in range(n_r)
        for b in range(n_c)
        if 0 <= a + rows < n_r and 0 <= b + cols < n_c
    ]
    return lax.ppermute(value, ("tx", "ty"), pairs)


def swap(parts, axes, groups):
    return lax.all_to_all(parts, axes, 0, 0, axis_index_groups=groups, tiled=True)


def device_groups():
    n_r, n_c = lax.axis_size("ty"), lax.axis_size("tx")
    depth = n_c // CORES
    plane = [
        [(z * CORES + c) * n_r + a for c in range(CORES) for a in range(n_r)] for z in range(depth)
    ]
    near = min(4, depth)

    def along(step, size):
        return [
            [(first + i * step) * CORES + c for i in range(size)]
            for c in range(CORES)
            for first in range(depth)
            if first // step % size == 0
        ]

    return plane, along(1, near), along(near, depth // near)


def sum_in_plane(value):
    plane, near, far = device_groups()
    parts = value.reshape(len(plane[0]), -1, value.shape[-1])
    return fold(swap(parts, ("tx", "ty"), plane), len(near[0]), "fold_plane")


def sum_along(parts):
    plane, near, far = device_groups()
    parts = fold(swap(parts, "tx", near), len(far[0]), "fold_near")
    parts = fold(swap(parts, "tx", far), len(plane[0]), "fold_far")
    parts = swap(parts, ("tx", "ty"), plane)
    return parts.reshape(2, -1, parts.shape[-1])


def fold(parts, copies, name):
    (out,) = call(fold_kernel, name, (), (), [(copies, *parts.shape[1:])], [], 1, 1)(parts)
    return out


def fold_kernel(parts, out, sems):
    mine = parts[0]
    for at in range(1, parts.shape[0]):
        mine += parts[at]
    for at in range(out.shape[0]):
        out[at] = mine


def dft_table(width):
    index = np.arange(width)
    angle = 2.0 * np.pi * ((index[:, None] * index[None, :]) % width) / width
    cos, sin = np.cos(angle) / np.sqrt(width), -np.sin(angle) / np.sqrt(width)
    table = np.block([[cos, sin], [-sin, cos]]).astype(np.float32)
    lead = table.astype(jnp.bfloat16)
    trail = (table - lead.astype(np.float32)).astype(jnp.bfloat16)
    return np.concatenate([lead, lead, trail], axis=0)


def transform(re, im, table):
    rows = jnp.concatenate([re, im], axis=1)
    lead = rows.astype(BF16)
    trail = (rows - lead.astype(F32)).astype(BF16)
    out = jnp.dot(
        jnp.concatenate([lead, trail, lead], axis=1), table[...], preferred_element_type=F32
    )
    width = re.shape[1]
    return out[:, :width], out[:, width:]


def turn(parts):
    return jnp.concatenate([jnp.transpose(part) for part in parts], axis=0)


def add_slots(org, count, ext, acc, probe_re, probe_im, total, inten, table):
    width = probe_re.shape[0]
    bottom = ext.shape[2] - width
    lanes = lax.broadcasted_iota(jnp.int32, (width, width), 1)

    def split(value):
        return [value[i * width : (i + 1) * width] for i in range(GROUP)]

    def some(step, carry):
        slots = [step * GROUP + i for i in range(GROUP)]
        rows, blocks, cols, masks = [], [], [], []
        weights = []
        for slot in slots:
            col = lax.rem(org[1, slot], (ext.shape[1] - 1) * width)
            rows.append(lax.rem(org[0, slot], bottom))
            blocks.append(col // width)
            cols.append(lax.rem(col, width))
            masks.append(lanes >= cols[-1])
            weights.append((slot < count).astype(F32))
        obj, prb = [], []
        for i in range(GROUP):
            where = pl.ds(rows[i], width)
            obj.append(
                [
                    jnp.where(masks[i], ext[p, blocks[i], where, :], ext[p, blocks[i] + 1, where, :])
                    for p in range(2)
                ]
            )
            prb.append([pltpu.roll(part, cols[i], 1) for part in (probe_re, probe_im)])
        wave_re = [p[0] * o[0] - p[1] * o[1] for p, o in zip(prb, obj)]
        wave_im = [p[0] * o[1] + p[1] * o[0] for p, o in zip(prb, obj)]
        half_re, half_im = transform(
            jnp.concatenate(wave_re, axis=0), jnp.concatenate(wave_im, axis=0), table
        )
        far_re, far_im = transform(turn(split(half_re)), turn(split(half_im)), table)
        seen = jnp.concatenate([inten[slot] for slot in slots], axis=0)
        misfit = far_re * far_re + far_im * far_im - seen
        misfit = jnp.concatenate([m * w for m, w in zip(split(misfit), weights)], axis=0)
        half_im, half_re = transform(misfit * far_im, misfit * far_re, table)
        back_im, back_re = transform(turn(split(half_im)), turn(split(half_re)), table)
        back_re, back_im = split(back_re), split(back_im)
        sums = [jnp.zeros((width, width), F32)] * 2
        for i in range(GROUP):
            where = pl.ds(rows[i], width)
            grad = (
                prb[i][0] * back_re[i] + prb[i][1] * back_im[i],
                prb[i][0] * back_im[i] - prb[i][1] * back_re[i],
            )
            for p in range(2):
                acc[p, blocks[i], where, :] += jnp.where(masks[i], grad[p], 0.0)
                acc[p, blocks[i] + 1, where, :] += jnp.where(masks[i], 0.0, grad[p])
            own = (
                obj[i][0] * back_re[i] + obj[i][1] * back_im[i],
                obj[i][0] * back_im[i] - obj[i][1] * back_re[i],
            )
            home = lax.rem(width - cols[i], width)
            sums = [s + pltpu.roll(o, home, 1) for s, o in zip(sums, own)]
        for p in range(2):
            total[p] += sums[p]
        return carry

    lax.fori_loop(0, (count + GROUP - 1) // GROUP, some, 0)


def peak_of(probe_re, probe_im):
    power = probe_re * probe_re + probe_im * probe_im
    top = jnp.max(jnp.max(power, axis=0, keepdims=True), axis=1, keepdims=True)
    return step_object / (top + 1e-6)


class Copies:
    def __init__(self, sems):
        self.sems, self.used = sems, 0

    def start(self, *pairs):
        out = []
        for source, target in pairs:
            out.append(pltpu.make_async_copy(source, target, self.sems.at[self.used]))
            out[-1].start()
            self.used += 1
        return out


def wait(copies):
    for copy in copies:
        copy.wait()


def pack_kernel(tile, below, right, corner, sems):
    width = right.shape[2]
    wait(
        Copies(sems).start(
            (tile.at[:, :width, :], below),
            (tile.at[:, :, :width], right),
            (tile.at[:, :width, :width], corner),
        )
    )


def prepare_kernel(
    tile, probe_in, inten_in, table_in, ext, probe, inten, table, inten_out, raw, sems
):
    width = ext.shape[3]
    bottom = tile.shape[1]
    copies = Copies(sems)
    first = copies.start((inten_in, raw))
    rest = copies.start((probe_in, probe), (table_in, table))
    for j in range(ext.shape[1] - 1):
        rest += copies.start((tile.at[:, :, pl.ds(j * width, width)], ext.at[:, j, :bottom]))
    wait(first)
    for slot in range(raw.shape[0]):
        inten[slot] = jnp.transpose(raw[slot])
    wait(rest + copies.start((inten, inten_out)))


def first_kernel(
    org, counts, ext_in, below, right, corner, probe, inten, table,
    ext, acc_0, acc_1, acc_2, up, down, total, acc, sems,
):
    n = ext.shape[1] - 1
    width = ext.shape[3]
    bottom = ext.shape[2] - width
    for p in range(2):
        for j in range(n):
            ext[p, j, bottom:] = below[p, :, j * width : (j + 1) * width]
        ext[p, n, :bottom] = right[p]
        ext[p, n, bottom:] = corner[p]
    acc[...] = jnp.zeros_like(acc)
    total[...] = jnp.zeros_like(total)
    add_slots(org, counts[0], ext, acc, probe[0], probe[1], total, inten, table)
    for p in range(2):
        for j, part in enumerate((acc_0, acc_1, acc_2)):
            part[p] = acc[p, j]
            up[p, j] = acc[p, j, :width]
            down[p, j] = acc[p, j, bottom:]


def corners_kernel(from_up, from_down, after, to_left, to_right, sems):
    del after
    last = from_up.shape[1] - 1
    for p in range(2):
        for at, block in enumerate((from_up, from_down)):
            to_left[p, at] = block[p, 0]
            to_right[p, at] = block[p, last]


def second_kernel(
    org, counts, ext, acc_0, acc_1, acc_2, from_left, from_right, from_up, from_down,
    more_left, more_right, probe_in, gathered, share, inten_in, table_in,
    obj_out, side_out, probe_out, total_out, right_out, down_out, corner_out,
    cur, acc, own, probe, total, inten, table, sems,
):
    n = cur.shape[1] - 1
    width = cur.shape[3]
    bottom = cur.shape[2] - width
    copies = Copies(sems)
    loads = copies.start((inten_in, inten), (table_in, table))
    scale = peak_of(probe_in[0], probe_in[1])
    mid = slice(width, bottom)
    for p in range(2):
        probe[p] = probe_in[p] - share[0] * gathered[p]
        rows = ((slice(0, width), from_up, 0), (mid, None, 0), (slice(bottom, None), from_down, 1))
        for j, (part, side, more) in enumerate(
            ((acc_0, from_left, more_left), (acc_1, None, None), (acc_2, from_right, more_right))
        ):
            for where, edge, at in rows:
                value = part[p, where]
                if side is not None:
                    value += side[p, where]
                if edge is not None:
                    value += edge[p, j]
                    if more is not None:
                        value += more[p, at]
                cur[p, j, where] = ext[p, j, where] - scale * value
    acc[...] = jnp.zeros_like(acc)
    total[...] = jnp.zeros_like(total)
    wait(loads)
    add_slots(org, counts[0], cur, acc, probe[0], probe[1], total, inten, table)
    stores = copies.start((total, total_out), (probe, probe_out))
    scale = peak_of(probe[0], probe[1])
    for p in range(2):
        for j in range(n):
            own[p, j] = cur[p, j, :bottom] - scale * acc[p, j, :bottom]
            acc[p, j, bottom:] = scale * acc[p, j, bottom:]
        acc[p, n] = scale * acc[p, n]
    stores += copies.start(
        (acc.at[:, n, :bottom], right_out), (acc.at[:, n, bottom:], corner_out),
        (acc.at[:, :n, bottom:], down_out), (own.at[:, 0], side_out),
    )
    for j in range(1, n):
        cols = pl.ds(j * width, width)
        stores += copies.start((own.at[:, j], obj_out.at[:, :, cols]))
    wait(stores)


def final_kernel(
    obj_in, side_in, probe_in, from_left, from_up, from_corner, gathered, share,
    obj_out, probe_out, side, top, probe, sems,
):
    width = side.shape[2]
    copies = Copies(sems)
    places = [pl.ds((j + 1) * width, width) for j in range(top.shape[1])]
    loads = copies.start((side_in, side), (probe_in, probe))
    for j, cols in enumerate(places):
        loads += copies.start((obj_in.at[:, :width, cols], top.at[:, j]))
    wait(loads)
    for p in range(2):
        side[p] -= from_left[p]
        side[p, :width] -= from_up[p, 0] + from_corner[p]
        for j in range(top.shape[1]):
            top[p, j] -= from_up[p, j + 1]
        probe[p] -= share[0] * gathered[p]
    stores = copies.start((side, obj_out.at[:, :, :width]), (probe, probe_out))
    for j, cols in enumerate(places):
        stores += copies.start((top.at[:, j], obj_out.at[:, :width, cols]))
    wait(stores)


def call(kernel, name, smem, far, outs, scratch, copies, mib, **more):
    kinds = {True: pltpu.HBM, False: pltpu.VMEM}

    def run(*operands):
        where = [pltpu.SMEM if at in smem else kinds[at in far] for at in range(len(operands))]
        held = [kinds[-1 - at in far] for at in range(len(outs))]
        operands = [
            value if space is pltpu.SMEM else pltpu.with_memory_space_constraint(value, space)
            for value, space in zip(operands, where)
        ]
        return pl.pallas_call(
            kernel,
            out_shape=[space(s, F32) if isinstance(s, tuple) else space(s.shape, s.dtype) for s, space in zip(outs, held)],
            in_specs=[pl.BlockSpec(memory_space=space) for space in where],
            out_specs=[pl.BlockSpec(memory_space=space) for space in held],
            scratch_shapes=[
                *(pltpu.VMEM(s, F32) if isinstance(s, tuple) else pltpu.VMEM(s.shape, s.dtype) for s in scratch),
                pltpu.SemaphoreType.DMA((copies,)),
            ],
            compiler_params=pltpu.CompilerParams(vmem_limit_bytes=mib * 1024 * 1024),
            name=name,
            **more,
        )(*operands)

    return run


def body(object_planes, probe, anchors, counts, intensity):
    rows, cols = object_planes.shape[1:]
    w = probe.shape[1]
    org = anchors[0, 0].T
    count = counts[0]
    inten = intensity[0, 0]
    table = jnp.asarray(dft_table(w))
    kept = jax.ShapeDtypeStruct(table.shape, table.dtype)
    slots = inten.shape
    n = cols // w
    tall, square = (2, rows + w, w), (2, w, w)
    blocks, strip = (2, n + 1, rows + w, w), (2, n + 1, w, w)
    share = jnp.full((1,), step_probe / (lax.axis_size("tx") * lax.axis_size("ty")), F32)

    below, right, corner = call(
        pack_kernel, "pack", (), (0,), [(2, w, cols), (2, rows, w), square], [], 3, 2
    )(object_planes)
    right, below, corner = shift(right, 0, -1), shift(below, -1, 0), shift(corner, -1, -1)
    ext, start, inten_near, table_near, inten = call(
        prepare_kernel, "prepare", (), (0, 1, 2, 3, -5),
        [blocks, square, slots, kept, slots], [slots], 6, 4,
    )(object_planes, probe, inten, table)
    ext, acc_0, acc_1, acc_2, up, down, total = call(
        first_kernel, "first_pass", (0, 1), (), [blocks, tall, tall, tall, strip, strip, square],
        [blocks], 1, 6, input_output_aliases={2: 0},
    )(org, count, ext, below, right, corner, start, inten_near, table_near)
    from_left, from_right = shift(acc_2, 0, 1), shift(acc_0, 0, -1)
    from_up, from_down = shift(down, 1, 0), shift(up, -1, 0)
    parts = sum_in_plane(total)
    to_left, to_right = call(
        corners_kernel, "corners", (), (), [(2, 2, w, w)] * 2, [], 1, 1
    )(from_up, from_down, parts)
    more_left, more_right = shift(to_right, 0, 1), shift(to_left, 0, -1)
    gathered = sum_along(parts)
    obj, side, current, total, to_right, to_down, to_corner = call(
        second_kernel, "second_pass", (0, 1, 14), (15, 16, *range(-7, 0)),
        [(2, rows, cols), (2, rows, w), square, square, (2, rows, w), (2, n, w, w), square],
        [blocks, blocks, (2, n, rows, w), square, square, slots, kept], n + 7, 9,
    )(
        org, count, ext, acc_0, acc_1, acc_2, from_left, from_right, from_up, from_down,
        more_left, more_right, start, gathered, share, inten, table,
    )
    from_left, from_up = shift(to_right, 0, 1), shift(to_down, 1, 0)
    from_corner = shift(to_corner, 1, 1)
    gathered = sum_along(sum_in_plane(total))
    obj, current = call(
        final_kernel, "finish", (7,), (0, 1, 2, -1, -2), [(2, rows, cols), square],
        [(2, rows, w), (2, n - 1, w, w), square], 2 * n + 2, 3, input_output_aliases={0: 0},
    )(obj, side, current, from_left, from_up, from_corner, gathered, share)
    return obj, current


def solution(mesh):
    return jax.shard_map(
        body,
        mesh=mesh,
        in_specs=(
            P(None, "ty", "tx"),
            P(),
            P("ty", "tx", None, None),
            P("ty", "tx"),
            P("ty", "tx", None, None, None),
        ),
        out_specs=(P(None, "ty", "tx"), P()),
        check_vma=False,
    )
```

```python
import jax
import jax.numpy as jnp
import numpy as np
from jax import lax
from jax.experimental import pallas as pl
from jax.experimental.pallas import tpu as pltpu
from jax.sharding import PartitionSpec as P

step_object = 1.0
step_probe = 1.0
GROUP = 2
CORES = 2
F32 = jnp.float32
BF16 = jnp.bfloat16


def shift(value, rows, cols):
    n_r, n_c = lax.axis_size("ty"), lax.axis_size("tx")
    if cols == 0:
        return lax.ppermute(
            value, "ty", [(a, a + rows) for a in range(n_r) if 0 <= a + rows < n_r]
        )
    if rows == 0:
        return lax.ppermute(
            value, "tx", [(b, b + cols) for b in range(n_c) if 0 <= b + cols < n_c]
        )
    pairs = [
        (b * n_r + a, (b + cols) * n_r + a + rows)
        for a in range(n_r)
        for b in range(n_c)
        if 0 <= a + rows < n_r and 0 <= b + cols < n_c
    ]
    return lax.ppermute(value, ("tx", "ty"), pairs)


def trade(value, axis, first):
    size = lax.axis_size(axis)
    pairs = []
    for one in range(first, size - 1, 2):
        pairs += [(one, one + 1), (one + 1, one)]
    return lax.ppermute(value, axis, pairs)


def gate_kernel(*refs):
    pass


def gate(values, after, far):
    whole = pl.BlockSpec(memory_space=pltpu.HBM if far else pl.ANY)
    if far:
        values = [pltpu.with_memory_space_constraint(value, pltpu.HBM) for value in values]
    return pl.pallas_call(
        gate_kernel,
        out_shape=[
            (pltpu.HBM if far else jax.ShapeDtypeStruct)(value.shape, value.dtype)
            for value in values
        ],
        in_specs=[whole] * len(values) + [pl.BlockSpec(memory_space=pl.ANY)],
        out_specs=[whole] * len(values),
        input_output_aliases={at: at for at in range(len(values))},
        name="gate",
    )(*values, after)


def swap(parts, axes, groups):
    return lax.all_to_all(parts, axes, 0, 0, axis_index_groups=groups, tiled=True)


def device_groups():
    n_r, n_c = lax.axis_size("ty"), lax.axis_size("tx")
    depth = n_c // CORES
    plane = [
        [(z * CORES + c) * n_r + a for c in range(CORES) for a in range(n_r)] for z in range(depth)
    ]
    near = min(4, depth)

    def along(step, size):
        return [
            [(first + i * step) * CORES + c for i in range(size)]
            for c in range(CORES)
            for first in range(depth)
            if first // step % size == 0
        ]

    return plane, along(1, near), along(near, depth // near)


def sum_in_plane(value):
    plane, near, far = device_groups()
    parts = value.reshape(len(plane[0]), -1, value.shape[-1])
    return fold(swap(parts, ("tx", "ty"), plane), len(near[0]), "fold_plane")


def sum_along(parts):
    plane, near, far = device_groups()
    parts = fold(swap(parts, "tx", near), len(far[0]), "fold_near")
    return fold(swap(parts, "tx", far), len(plane[0]), "fold_far")


def collect(parts):
    parts = swap(parts, ("tx", "ty"), device_groups()[0])
    return parts.reshape(2, -1, parts.shape[-1])


def fold(parts, copies, name):
    (out,) = call(fold_kernel, name, (), (), [(copies, *parts.shape[1:])], [], 1, 1)(parts)
    return out


def fold_kernel(parts, out, sems):
    mine = parts[0]
    for at in range(1, parts.shape[0]):
        mine += parts[at]
    for at in range(out.shape[0]):
        out[at] = mine


def dft_table(width):
    index = np.arange(width)
    angle = 2.0 * np.pi * ((index[:, None] * index[None, :]) % width) / width
    cos, sin = np.cos(angle) / np.sqrt(width), -np.sin(angle) / np.sqrt(width)
    table = np.block([[cos, sin], [-sin, cos]]).astype(np.float32)
    lead = table.astype(jnp.bfloat16)
    trail = (table - lead.astype(np.float32)).astype(jnp.bfloat16)
    return np.concatenate([lead, lead, trail], axis=0)


def transform(re, im, table):
    rows = jnp.concatenate([re, im], axis=1)
    lead = rows.astype(BF16)
    trail = (rows - lead.astype(F32)).astype(BF16)
    out = jnp.dot(
        jnp.concatenate([lead, trail, lead], axis=1), table[...], preferred_element_type=F32
    )
    width = re.shape[1]
    return out[:, :width], out[:, width:]


def turn(parts):
    return jnp.concatenate([jnp.transpose(part) for part in parts], axis=0)


def add_slots(org, count, ext, acc, probe_re, probe_im, total, inten, table):
    width = probe_re.shape[0]
    bottom = ext.shape[2] - width
    lanes = lax.broadcasted_iota(jnp.int32, (width, width), 1)

    def split(value):
        return [value[i * width : (i + 1) * width] for i in range(GROUP)]

    def some(step, carry):
        slots = [step * GROUP + i for i in range(GROUP)]
        rows, blocks, cols, masks = [], [], [], []
        weights = []
        for slot in slots:
            col = lax.rem(org[1, slot], (ext.shape[1] - 1) * width)
            rows.append(lax.rem(org[0, slot], bottom))
            blocks.append(col // width)
            cols.append(lax.rem(col, width))
            masks.append(lanes >= cols[-1])
            weights.append((slot < count).astype(F32))
        obj, prb = [], []
        for i in range(GROUP):
            where = pl.ds(rows[i], width)
            obj.append(
                [
                    jnp.where(masks[i], ext[p, blocks[i], where, :], ext[p, blocks[i] + 1, where, :])
                    for p in range(2)
                ]
            )
            prb.append([pltpu.roll(part, cols[i], 1) for part in (probe_re, probe_im)])
        wave_re = [p[0] * o[0] - p[1] * o[1] for p, o in zip(prb, obj)]
        wave_im = [p[0] * o[1] + p[1] * o[0] for p, o in zip(prb, obj)]
        half_re, half_im = transform(
            jnp.concatenate(wave_re, axis=0), jnp.concatenate(wave_im, axis=0), table
        )
        far_re, far_im = transform(turn(split(half_re)), turn(split(half_im)), table)
        seen = jnp.concatenate([inten[slot] for slot in slots], axis=0)
        misfit = far_re * far_re + far_im * far_im - seen
        misfit = jnp.concatenate([m * w for m, w in zip(split(misfit), weights)], axis=0)
        half_im, half_re = transform(misfit * far_im, misfit * far_re, table)
        back_im, back_re = transform(turn(split(half_im)), turn(split(half_re)), table)
        back_re, back_im = split(back_re), split(back_im)
        sums = [jnp.zeros((width, width), F32)] * 2
        for i in range(GROUP):
            where = pl.ds(rows[i], width)
            grad = (
                prb[i][0] * back_re[i] + prb[i][1] * back_im[i],
                prb[i][0] * back_im[i] - prb[i][1] * back_re[i],
            )
            for p in range(2):
                acc[p, blocks[i], where, :] += jnp.where(masks[i], grad[p], 0.0)
                acc[p, blocks[i] + 1, where, :] += jnp.where(masks[i], 0.0, grad[p])
            own = (
                obj[i][0] * back_re[i] + obj[i][1] * back_im[i],
                obj[i][0] * back_im[i] - obj[i][1] * back_re[i],
            )
            home = lax.rem(width - cols[i], width)
            sums = [s + pltpu.roll(o, home, 1) for s, o in zip(sums, own)]
        for p in range(2):
            total[p] += sums[p]
        return carry

    lax.fori_loop(0, (count + GROUP - 1) // GROUP, some, 0)


def peak_of(probe_re, probe_im):
    power = probe_re * probe_re + probe_im * probe_im
    top = jnp.max(jnp.max(power, axis=0, keepdims=True), axis=1, keepdims=True)
    return step_object / (top + 1e-6)


class Copies:
    def __init__(self, sems):
        self.sems, self.used = sems, 0

    def start(self, *pairs):
        out = []
        for source, target in pairs:
            out.append(pltpu.make_async_copy(source, target, self.sems.at[self.used]))
            out[-1].start()
            self.used += 1
        return out


def wait(copies):
    for copy in copies:
        copy.wait()


def pack_kernel(tile, below, right, corner, sems):
    width = right.shape[2]
    wait(
        Copies(sems).start(
            (tile.at[:, :width, :], below),
            (tile.at[:, :, :width], right),
            (tile.at[:, :width, :width], corner),
        )
    )


def prepare_kernel(
    tile, probe_in, inten_in, table_in, ext, probe, inten, table, inten_out, raw, sems
):
    width = ext.shape[3]
    bottom = tile.shape[1]
    copies = Copies(sems)
    first = copies.start((inten_in, raw))
    rest = copies.start((probe_in, probe), (table_in, table))
    for j in range(ext.shape[1] - 1):
        rest += copies.start((tile.at[:, :, pl.ds(j * width, width)], ext.at[:, j, :bottom]))
    wait(first)
    for slot in range(raw.shape[0]):
        inten[slot] = jnp.transpose(raw[slot])
    wait(rest + copies.start((inten, inten_out)))


def partners(odd, n, bottom):
    block_a = jnp.where(odd[0] == 0, n, 0)
    row_c = pl.multiple_of(jnp.where(odd[1] == 0, bottom, 0), 128)
    return block_a, n - block_a, row_c, pl.multiple_of(bottom - row_c, 128)


def first_kernel(
    org, counts, odd, ext_in, below, right, corner, probe, inten, table,
    ext, side_a, side_b, inner, rows_c, rows_d, total, acc, sems,
):
    n = ext.shape[1] - 1
    width = ext.shape[3]
    bottom = ext.shape[2] - width
    for p in range(2):
        for j in range(n):
            ext[p, j, :bottom] = ext_in[p, j, :bottom]
            ext[p, j, bottom:] = below[p, :, j * width : (j + 1) * width]
        ext[p, n, :bottom] = right[p]
        ext[p, n, bottom:] = corner[p]
    acc[...] = jnp.zeros_like(acc)
    total[...] = jnp.zeros_like(total)
    add_slots(org, counts[0], ext, acc, probe[0], probe[1], total, inten, table)
    block_a, block_b, row_c, row_d = partners(odd, n, bottom)
    for p in range(2):
        side_a[p] = acc[p, block_a]
        side_b[p] = acc[p, block_b]
        inner[p] = acc[p, 1]
        for j in range(n + 1):
            rows_c[p, j] = acc[p, j, pl.ds(row_c, width), :]
            rows_d[p, j] = acc[p, j, pl.ds(row_d, width), :]


def corners_kernel(odd, from_c, from_d, after, to_a, to_b, sems):
    del after
    n = from_c.shape[1] - 1
    block_a, block_b, _, _ = partners(odd, n, 0)
    for p in range(2):
        for at, block in enumerate((from_c, from_d)):
            to_a[p, at] = block[p, block_a]
            to_b[p, at] = block[p, block_b]


def second_kernel(
    org, counts, odd, ext, side_a, side_b, inner, from_a, from_b, from_c, from_d,
    more_a, more_b, probe_in, gathered, share, inten_in, table_in,
    obj_out, side_out, probe_out, total_out, right_out, down_out, corner_out,
    cur, acc, own, probe, total, inten, table, sems,
):
    n = cur.shape[1] - 1
    width = cur.shape[3]
    bottom = cur.shape[2] - width
    copies = Copies(sems)
    loads = copies.start((inten_in, inten), (table_in, table))
    scale = peak_of(probe_in[0], probe_in[1])
    block_a, block_b, row_c, row_d = partners(odd, n, bottom)
    where_c, where_d = pl.ds(row_c, width), pl.ds(row_d, width)
    for p in range(2):
        probe[p] = probe_in[p] - share[0] * gathered[p]
        cur[p, 1] = ext[p, 1] - scale * inner[p]
        cur[p, block_a] = ext[p, block_a] - scale * (side_a[p] + from_a[p])
        cur[p, block_b] = ext[p, block_b] - scale * (side_b[p] + from_b[p])
        for j in range(n + 1):
            cur[p, j, where_c, :] -= scale * from_c[p, j]
            cur[p, j, where_d, :] -= scale * from_d[p, j]
        for block, more in ((block_a, more_a), (block_b, more_b)):
            cur[p, block, where_c, :] -= scale * more[p, 0]
            cur[p, block, where_d, :] -= scale * more[p, 1]
    acc[...] = jnp.zeros_like(acc)
    total[...] = jnp.zeros_like(total)
    wait(loads)
    add_slots(org, counts[0], cur, acc, probe[0], probe[1], total, inten, table)
    stores = copies.start((total, total_out), (probe, probe_out))
    scale = peak_of(probe[0], probe[1])
    for p in range(2):
        for j in range(n):
            own[p, j] = cur[p, j, :bottom] - scale * acc[p, j, :bottom]
            acc[p, j, bottom:] = scale * acc[p, j, bottom:]
        acc[p, n] = scale * acc[p, n]
    stores += copies.start(
        (acc.at[:, n, :bottom], right_out), (acc.at[:, n, bottom:], corner_out),
        (acc.at[:, :n, bottom:], down_out), (own.at[:, 0], side_out),
    )
    for j in range(1, n):
        cols = pl.ds(j * width, width)
        stores += copies.start((own.at[:, j], obj_out.at[:, :, cols]))
    wait(stores)


def final_kernel(
    obj_in, side_in, probe_in, from_left, from_up, from_corner, gathered, share,
    obj_out, probe_out, side, top, probe, sems,
):
    width = side.shape[2]
    copies = Copies(sems)
    places = [pl.ds((j + 1) * width, width) for j in range(top.shape[1])]
    loads = copies.start((side_in, side), (probe_in, probe))
    for j, cols in enumerate(places):
        loads += copies.start((obj_in.at[:, :width, cols], top.at[:, j]))
    wait(loads)
    for p in range(2):
        side[p] -= from_left[p]
        side[p, :width] -= from_up[p, 0] + from_corner[p]
        for j in range(top.shape[1]):
            top[p, j] -= from_up[p, j + 1]
        probe[p] -= share[0] * gathered[p]
    stores = copies.start((side, obj_out.at[:, :, :width]), (probe, probe_out))
    for j, cols in enumerate(places):
        stores += copies.start((top.at[:, j], obj_out.at[:, :width, cols]))
    wait(stores)


def call(kernel, name, smem, far, outs, scratch, copies, mib, **more):
    kinds = {True: pltpu.HBM, False: pltpu.VMEM}

    def run(*operands):
        where = [pltpu.SMEM if at in smem else kinds[at in far] for at in range(len(operands))]
        held = [kinds[-1 - at in far] for at in range(len(outs))]
        operands = [
            value if space is pltpu.SMEM else pltpu.with_memory_space_constraint(value, space)
            for value, space in zip(operands, where)
        ]
        return pl.pallas_call(
            kernel,
            out_shape=[space(s, F32) if isinstance(s, tuple) else space(s.shape, s.dtype) for s, space in zip(outs, held)],
            in_specs=[pl.BlockSpec(memory_space=space) for space in where],
            out_specs=[pl.BlockSpec(memory_space=space) for space in held],
            scratch_shapes=[
                *(pltpu.VMEM(s, F32) if isinstance(s, tuple) else pltpu.VMEM(s.shape, s.dtype) for s in scratch),
                pltpu.SemaphoreType.DMA((copies,)),
            ],
            compiler_params=pltpu.CompilerParams(vmem_limit_bytes=mib * 1024 * 1024),
            name=name,
            **more,
        )(*operands)

    return run


def body(object_planes, probe, anchors, counts, intensity):
    rows, cols = object_planes.shape[1:]
    w = probe.shape[1]
    org = anchors[0, 0].T
    count = counts[0]
    inten = intensity[0, 0]
    table = jnp.asarray(dft_table(w))
    kept = jax.ShapeDtypeStruct(table.shape, table.dtype)
    slots = inten.shape
    n = cols // w
    tall, square = (2, rows + w, w), (2, w, w)
    blocks, strip = (2, n + 1, rows + w, w), (2, n + 1, w, w)
    share = jnp.full((1,), step_probe / (lax.axis_size("tx") * lax.axis_size("ty")), F32)

    below, right, corner = call(
        pack_kernel, "pack", (), (0,), [(2, w, cols), (2, rows, w), square], [], 3, 2
    )(object_planes)
    right, below, corner = shift(right, 0, -1), shift(below, -1, 0), shift(corner, -1, -1)
    ext, start, inten_near, table_near, inten = call(
        prepare_kernel, "prepare", (), (0, 1, 2, 3, -5),
        [blocks, square, slots, kept, slots], [slots], 6, 4,
    )(object_planes, probe, inten, table)
    odd = jnp.stack([lax.axis_index("tx") % 2, lax.axis_index("ty") % 2]).astype(jnp.int32)
    ext, side_a, side_b, inner, rows_c, rows_d, total = call(
        first_kernel, "first_pass", (0, 1, 2), (),
        [blocks, tall, tall, tall, strip, strip, square], [blocks], 1, 6,
    )(org, count, odd, ext, below, right, corner, start, inten_near, table_near)
    parts = sum_in_plane(total)
    side_a, side_b, rows_c, rows_d = gate((side_a, side_b, rows_c, rows_d), parts, False)
    from_c, from_d = trade(rows_c, "ty", 0), trade(rows_d, "ty", 1)
    from_a, from_b = trade(side_a, "tx", 0), trade(side_b, "tx", 1)
    parts = sum_along(parts)
    to_a, to_b = call(corners_kernel, "corners", (0,), (), [(2, 2, w, w)] * 2, [], 1, 1)(
        odd, from_c, from_d, parts
    )
    more_a, more_b = trade(to_a, "tx", 0), trade(to_b, "tx", 1)
    gathered = collect(parts)
    obj, side, current, total, to_right, to_down, to_corner = call(
        second_kernel, "second_pass", (0, 1, 2, 15), (16, 17, *range(-7, 0)),
        [(2, rows, cols), (2, rows, w), square, square, (2, rows, w), (2, n, w, w), square],
        [blocks, blocks, (2, n, rows, w), square, square, slots, kept], n + 7, 9,
    )(
        org, count, odd, ext, side_a, side_b, inner, from_a, from_b, from_c, from_d,
        more_a, more_b, start, gathered, share, inten, table,
    )
    parts = sum_along(sum_in_plane(total))
    to_right, to_down, to_corner = gate((to_right, to_down, to_corner), parts, True)
    from_left, from_up = shift(to_right, 0, 1), shift(to_down, 1, 0)
    from_corner = shift(to_corner, 1, 1)
    gathered = collect(parts)
    obj, current = call(
        final_kernel, "finish", (7,), (0, 1, 2, -1, -2), [(2, rows, cols), square],
        [(2, rows, w), (2, n - 1, w, w), square], 2 * n + 2, 3, input_output_aliases={0: 0},
    )(obj, side, current, from_left, from_up, from_corner, gathered, share)
    return obj, current


def solution(mesh):
    return jax.shard_map(
        body,
        mesh=mesh,
        in_specs=(
            P(None, "ty", "tx"),
            P(),
            P("ty", "tx", None, None),
            P("ty", "tx"),
            P("ty", "tx", None, None, None),
        ),
        out_specs=(P(None, "ty", "tx"), P()),
        check_vma=False,
    )
```

```python
import jax
import jax.numpy as jnp
import numpy as np
from jax import lax
from jax.experimental import pallas as pl
from jax.experimental.pallas import tpu as pltpu
from jax.sharding import PartitionSpec as P

step_object = 1.0
step_probe = 1.0
GROUP = 2
CORES = 2
F32 = jnp.float32
BF16 = jnp.bfloat16


def shift(value, rows, cols):
    n_r, n_c = lax.axis_size("ty"), lax.axis_size("tx")
    if cols == 0:
        return lax.ppermute(
            value, "ty", [(a, a + rows) for a in range(n_r) if 0 <= a + rows < n_r]
        )
    if rows == 0:
        return lax.ppermute(
            value, "tx", [(b, b + cols) for b in range(n_c) if 0 <= b + cols < n_c]
        )
    pairs = [
        (b * n_r + a, (b + cols) * n_r + a + rows)
        for a in range(n_r)
        for b in range(n_c)
        if 0 <= a + rows < n_r and 0 <= b + cols < n_c
    ]
    return lax.ppermute(value, ("tx", "ty"), pairs)


def swap(parts, axes, groups):
    return lax.all_to_all(parts, axes, 0, 0, axis_index_groups=groups, tiled=True)


def device_groups():
    n_r, n_c = lax.axis_size("ty"), lax.axis_size("tx")
    depth = n_c // CORES
    plane = [
        [(z * CORES + c) * n_r + a for c in range(CORES) for a in range(n_r)] for z in range(depth)
    ]
    return plane, [[z * CORES + c for z in range(depth)] for c in range(CORES)]


def sum_in_plane(value):
    plane, line = device_groups()
    parts = value.reshape(len(plane[0]), -1, value.shape[-1])
    return fold(swap(parts, ("tx", "ty"), plane), len(line[0]), "fold_plane")


def sum_along(parts):
    plane, line = device_groups()
    parts = fold(swap(parts, "tx", line), len(plane[0]), "fold_line")
    parts = swap(parts, ("tx", "ty"), plane)
    return parts.reshape(2, -1, parts.shape[-1])


def fold(parts, copies, name):
    (out,) = call(fold_kernel, name, (), (), [(copies, *parts.shape[1:])], [], 1, 1)(parts)
    return out


def fold_kernel(parts, out, sems):
    mine = parts[0]
    for at in range(1, parts.shape[0]):
        mine += parts[at]
    for at in range(out.shape[0]):
        out[at] = mine


def dft_table(width):
    index = np.arange(width)
    angle = 2.0 * np.pi * ((index[:, None] * index[None, :]) % width) / width
    cos, sin = np.cos(angle) / np.sqrt(width), -np.sin(angle) / np.sqrt(width)
    table = np.block([[cos, sin], [-sin, cos]]).astype(np.float32)
    lead = table.astype(jnp.bfloat16)
    trail = (table - lead.astype(np.float32)).astype(jnp.bfloat16)
    return np.concatenate([lead, lead, trail], axis=0)


def transform(re, im, table):
    rows = jnp.concatenate([re, im], axis=1)
    lead = rows.astype(BF16)
    trail = (rows - lead.astype(F32)).astype(BF16)
    out = jnp.dot(
        jnp.concatenate([lead, trail, lead], axis=1), table[...], preferred_element_type=F32
    )
    width = re.shape[1]
    return out[:, :width], out[:, width:]


def turn(parts):
    return jnp.concatenate([jnp.transpose(part) for part in parts], axis=0)


def add_slots(org, count, ext, acc, probe_re, probe_im, total, inten, table):
    width = probe_re.shape[0]
    bottom = ext.shape[2] - width
    lanes = lax.broadcasted_iota(jnp.int32, (width, width), 1)

    def split(value):
        return [value[i * width : (i + 1) * width] for i in range(GROUP)]

    def some(step, carry):
        slots = [step * GROUP + i for i in range(GROUP)]
        rows, blocks, cols, masks = [], [], [], []
        weights = []
        for slot in slots:
            col = lax.rem(org[1, slot], (ext.shape[1] - 1) * width)
            rows.append(lax.rem(org[0, slot], bottom))
            blocks.append(col // width)
            cols.append(lax.rem(col, width))
            masks.append(lanes >= cols[-1])
            weights.append((slot < count).astype(F32))
        obj, prb = [], []
        for i in range(GROUP):
            where = pl.ds(rows[i], width)
            obj.append(
                [
                    jnp.where(masks[i], ext[p, blocks[i], where, :], ext[p, blocks[i] + 1, where, :])
                    for p in range(2)
                ]
            )
            prb.append([pltpu.roll(part, cols[i], 1) for part in (probe_re, probe_im)])
        wave_re = [p[0] * o[0] - p[1] * o[1] for p, o in zip(prb, obj)]
        wave_im = [p[0] * o[1] + p[1] * o[0] for p, o in zip(prb, obj)]
        half_re, half_im = transform(
            jnp.concatenate(wave_re, axis=0), jnp.concatenate(wave_im, axis=0), table
        )
        far_re, far_im = transform(turn(split(half_re)), turn(split(half_im)), table)
        seen = jnp.concatenate([inten[slot] for slot in slots], axis=0)
        misfit = far_re * far_re + far_im * far_im - seen
        misfit = jnp.concatenate([m * w for m, w in zip(split(misfit), weights)], axis=0)
        half_im, half_re = transform(misfit * far_im, misfit * far_re, table)
        back_im, back_re = transform(turn(split(half_im)), turn(split(half_re)), table)
        back_re, back_im = split(back_re), split(back_im)
        sums = [jnp.zeros((width, width), F32)] * 2
        for i in range(GROUP):
            where = pl.ds(rows[i], width)
            grad = (
                prb[i][0] * back_re[i] + prb[i][1] * back_im[i],
                prb[i][0] * back_im[i] - prb[i][1] * back_re[i],
            )
            for p in range(2):
                acc[p, blocks[i], where, :] += jnp.where(masks[i], grad[p], 0.0)
                acc[p, blocks[i] + 1, where, :] += jnp.where(masks[i], 0.0, grad[p])
            own = (
                obj[i][0] * back_re[i] + obj[i][1] * back_im[i],
                obj[i][0] * back_im[i] - obj[i][1] * back_re[i],
            )
            home = lax.rem(width - cols[i], width)
            sums = [s + pltpu.roll(o, home, 1) for s, o in zip(sums, own)]
        for p in range(2):
            total[p] += sums[p]
        return carry

    lax.fori_loop(0, (count + GROUP - 1) // GROUP, some, 0)


def peak_of(probe_re, probe_im):
    power = probe_re * probe_re + probe_im * probe_im
    top = jnp.max(jnp.max(power, axis=0, keepdims=True), axis=1, keepdims=True)
    return step_object / (top + 1e-6)


class Copies:
    def __init__(self, sems):
        self.sems, self.used = sems, 0

    def start(self, *pairs):
        out = []
        for source, target in pairs:
            out.append(pltpu.make_async_copy(source, target, self.sems.at[self.used]))
            out[-1].start()
            self.used += 1
        return out


def wait(copies):
    for copy in copies:
        copy.wait()


def pack_kernel(tile, below, right, corner, sems):
    width = right.shape[2]
    wait(
        Copies(sems).start(
            (tile.at[:, :width, :], below),
            (tile.at[:, :, :width], right),
            (tile.at[:, :width, :width], corner),
        )
    )


def prepare_kernel(
    tile, probe_in, inten_in, table_in, ext, probe, inten, table, inten_out, raw, sems
):
    width = ext.shape[3]
    bottom = tile.shape[1]
    copies = Copies(sems)
    first = copies.start((inten_in, raw))
    rest = copies.start((probe_in, probe), (table_in, table))
    for j in range(ext.shape[1] - 1):
        rest += copies.start((tile.at[:, :, pl.ds(j * width, width)], ext.at[:, j, :bottom]))
    wait(first)
    for slot in range(raw.shape[0]):
        inten[slot] = jnp.transpose(raw[slot])
    wait(rest + copies.start((inten, inten_out)))


def first_kernel(
    org, counts, ext_in, below, right, corner, probe, inten, table,
    ext, acc_0, acc_1, acc_2, total, acc, sems,
):
    n = ext.shape[1] - 1
    width = ext.shape[3]
    bottom = ext.shape[2] - width
    for p in range(2):
        for j in range(n):
            ext[p, j, :bottom] = ext_in[p, j, :bottom]
            ext[p, j, bottom:] = below[p, :, j * width : (j + 1) * width]
        ext[p, n, :bottom] = right[p]
        ext[p, n, bottom:] = corner[p]
    acc[...] = jnp.zeros_like(acc)
    total[...] = jnp.zeros_like(total)
    add_slots(org, counts[0], ext, acc, probe[0], probe[1], total, inten, table)
    for p in range(2):
        for j, part in enumerate((acc_0, acc_1, acc_2)):
            part[p] = acc[p, j]


def strips_kernel(acc_0, acc_1, acc_2, from_left, from_right, after, up, down, sems):
    del after
    width = up.shape[2]
    bottom = acc_0.shape[1] - width
    for p in range(2):
        for rows, block in ((slice(0, width), up), (slice(bottom, None), down)):
            block[p, 0] = acc_0[p, rows] + from_left[p, rows]
            block[p, 1] = acc_1[p, rows]
            block[p, 2] = acc_2[p, rows] + from_right[p, rows]


def second_kernel(
    org, counts, ext, acc_0, acc_1, acc_2, from_left, from_right, from_up, from_down,
    probe_in, gathered, share, inten_in, table_in,
    obj_out, side_out, probe_out, total_out, right_out, down_out, corner_out,
    cur, acc, own, probe, total, inten, table, sems,
):
    n = cur.shape[1] - 1
    width = cur.shape[3]
    bottom = cur.shape[2] - width
    copies = Copies(sems)
    loads = copies.start((inten_in, inten), (table_in, table))
    scale = peak_of(probe_in[0], probe_in[1])
    mid = slice(width, bottom)
    for p in range(2):
        probe[p] = probe_in[p] - share[0] * gathered[p]
        rows = ((slice(0, width), from_up), (mid, None), (slice(bottom, None), from_down))
        for j, (part, side) in enumerate(
            ((acc_0, from_left), (acc_1, None), (acc_2, from_right))
        ):
            for where, edge in rows:
                value = part[p, where]
                if side is not None:
                    value += side[p, where]
                if edge is not None:
                    value += edge[p, j]
                cur[p, j, where] = ext[p, j, where] - scale * value
    acc[...] = jnp.zeros_like(acc)
    total[...] = jnp.zeros_like(total)
    wait(loads)
    add_slots(org, counts[0], cur, acc, probe[0], probe[1], total, inten, table)
    stores = copies.start((total, total_out), (probe, probe_out))
    scale = peak_of(probe[0], probe[1])
    for p in range(2):
        for j in range(n):
            own[p, j] = cur[p, j, :bottom] - scale * acc[p, j, :bottom]
            acc[p, j, bottom:] = scale * acc[p, j, bottom:]
        acc[p, n] = scale * acc[p, n]
    stores += copies.start(
        (acc.at[:, n, :bottom], right_out), (acc.at[:, n, bottom:], corner_out),
        (acc.at[:, :n, bottom:], down_out), (own.at[:, 0], side_out),
    )
    for j in range(1, n):
        cols = pl.ds(j * width, width)
        stores += copies.start((own.at[:, j], obj_out.at[:, :, cols]))
    wait(stores)


def final_kernel(
    obj_in, side_in, probe_in, from_left, from_up, from_corner, gathered, share,
    obj_out, probe_out, side, top, probe, sems,
):
    width = side.shape[2]
    copies = Copies(sems)
    places = [pl.ds((j + 1) * width, width) for j in range(top.shape[1])]
    loads = copies.start((side_in, side), (probe_in, probe))
    for j, cols in enumerate(places):
        loads += copies.start((obj_in.at[:, :width, cols], top.at[:, j]))
    wait(loads)
    for p in range(2):
        side[p] -= from_left[p]
        side[p, :width] -= from_up[p, 0] + from_corner[p]
        for j in range(top.shape[1]):
            top[p, j] -= from_up[p, j + 1]
        probe[p] -= share[0] * gathered[p]
    stores = copies.start((side, obj_out.at[:, :, :width]), (probe, probe_out))
    for j, cols in enumerate(places):
        stores += copies.start((top.at[:, j], obj_out.at[:, :width, cols]))
    wait(stores)


def call(kernel, name, smem, far, outs, scratch, copies, mib, **more):
    kinds = {True: pltpu.HBM, False: pltpu.VMEM}

    def run(*operands):
        where = [pltpu.SMEM if at in smem else kinds[at in far] for at in range(len(operands))]
        held = [kinds[-1 - at in far] for at in range(len(outs))]
        operands = [
            value if space is pltpu.SMEM else pltpu.with_memory_space_constraint(value, space)
            for value, space in zip(operands, where)
        ]
        return pl.pallas_call(
            kernel,
            out_shape=[space(s, F32) if isinstance(s, tuple) else space(s.shape, s.dtype) for s, space in zip(outs, held)],
            in_specs=[pl.BlockSpec(memory_space=space) for space in where],
            out_specs=[pl.BlockSpec(memory_space=space) for space in held],
            scratch_shapes=[
                *(pltpu.VMEM(s, F32) if isinstance(s, tuple) else pltpu.VMEM(s.shape, s.dtype) for s in scratch),
                pltpu.SemaphoreType.DMA((copies,)),
            ],
            compiler_params=pltpu.CompilerParams(vmem_limit_bytes=mib * 1024 * 1024),
            name=name,
            **more,
        )(*operands)

    return run


def body(object_planes, probe, anchors, counts, intensity):
    rows, cols = object_planes.shape[1:]
    w = probe.shape[1]
    org = anchors[0, 0].T
    count = counts[0]
    inten = intensity[0, 0]
    table = jnp.asarray(dft_table(w))
    kept = jax.ShapeDtypeStruct(table.shape, table.dtype)
    slots = inten.shape
    n = cols // w
    tall, square = (2, rows + w, w), (2, w, w)
    blocks, strip = (2, n + 1, rows + w, w), (2, n + 1, w, w)
    share = jnp.full((1,), step_probe / (lax.axis_size("tx") * lax.axis_size("ty")), F32)

    below, right, corner = call(
        pack_kernel, "pack", (), (0,), [(2, w, cols), (2, rows, w), square], [], 3, 2
    )(object_planes)
    right, below, corner = shift(right, 0, -1), shift(below, -1, 0), shift(corner, -1, -1)
    ext, start, inten_near, table_near, inten = call(
        prepare_kernel, "prepare", (), (0, 1, 2, 3, -5),
        [blocks, square, slots, kept, slots], [slots], 6, 4,
    )(object_planes, probe, inten, table)
    ext, acc_0, acc_1, acc_2, total = call(
        first_kernel, "first_pass", (0, 1), (), [blocks, tall, tall, tall, square], [blocks], 1, 6
    )(org, count, ext, below, right, corner, start, inten_near, table_near)
    from_left, from_right = shift(acc_2, 0, 1), shift(acc_0, 0, -1)
    parts = sum_in_plane(total)
    up, down = call(strips_kernel, "strips", (), (), [strip, strip], [], 1, 1)(
        acc_0, acc_1, acc_2, from_left, from_right, parts
    )
    from_up, from_down = shift(down, 1, 0), shift(up, -1, 0)
    gathered = sum_along(parts)
    obj, side, current, total, to_right, to_down, to_corner = call(
        second_kernel, "second_pass", (0, 1, 12), (13, 14, *range(-7, 0)),
        [(2, rows, cols), (2, rows, w), square, square, (2, rows, w), (2, n, w, w), square],
        [blocks, blocks, (2, n, rows, w), square, square, slots, kept], n + 7, 9,
    )(
        org, count, ext, acc_0, acc_1, acc_2, from_left, from_right, from_up, from_down,
        start, gathered, share, inten, table,
    )
    from_left, from_up = shift(to_right, 0, 1), shift(to_down, 1, 0)
    from_corner = shift(to_corner, 1, 1)
    gathered = sum_along(sum_in_plane(total))
    obj, current = call(
        final_kernel, "finish", (7,), (0, 1, 2, -1, -2), [(2, rows, cols), square],
        [(2, rows, w), (2, n - 1, w, w), square], 2 * n + 2, 3, input_output_aliases={0: 0},
    )(obj, side, current, from_left, from_up, from_corner, gathered, share)
    return obj, current


def solution(mesh):
    return jax.shard_map(
        body,
        mesh=mesh,
        in_specs=(
            P(None, "ty", "tx"),
            P(),
            P("ty", "tx", None, None),
            P("ty", "tx"),
            P("ty", "tx", None, None, None),
        ),
        out_specs=(P(None, "ty", "tx"), P()),
        check_vma=False,
    )
```

```python
import jax
import jax.numpy as jnp
import numpy as np
from jax import lax
from jax.experimental import pallas as pl
from jax.experimental.pallas import tpu as pltpu
from jax.sharding import PartitionSpec as P

step_object = 1.0
step_probe = 1.0
GROUP = 2
CORES = 2
F32 = jnp.float32
BF16 = jnp.bfloat16


def shift(value, rows, cols):
    n_r, n_c = lax.axis_size("ty"), lax.axis_size("tx")
    if cols == 0:
        return lax.ppermute(
            value, "ty", [(a, a + rows) for a in range(n_r) if 0 <= a + rows < n_r]
        )
    if rows == 0:
        return lax.ppermute(
            value, "tx", [(b, b + cols) for b in range(n_c) if 0 <= b + cols < n_c]
        )
    pairs = [
        (b * n_r + a, (b + cols) * n_r + a + rows)
        for a in range(n_r)
        for b in range(n_c)
        if 0 <= a + rows < n_r and 0 <= b + cols < n_c
    ]
    return lax.ppermute(value, ("tx", "ty"), pairs)


def swap(parts, axes, groups):
    return lax.all_to_all(parts, axes, 0, 0, axis_index_groups=groups, tiled=True)


def device_groups():
    n_r, n_c = lax.axis_size("ty"), lax.axis_size("tx")
    depth = n_c // CORES
    plane = [
        [(z * CORES + c) * n_r + a for c in range(CORES) for a in range(n_r)] for z in range(depth)
    ]
    return plane, [[z * CORES + c for z in range(depth)] for c in range(CORES)]


def sum_in_plane(value):
    plane, line = device_groups()
    parts = value.reshape(len(plane[0]), -1, value.shape[-1])
    return fold(swap(parts, ("tx", "ty"), plane), len(line[0]), "fold_plane")


def sum_along(parts, *after):
    plane, line = device_groups()
    return fold(swap(parts, "tx", line), len(plane[0]), "fold_line", *after)


def collect(parts):
    parts = swap(parts, ("tx", "ty"), device_groups()[0])
    return parts.reshape(2, -1, parts.shape[-1])


def fold(parts, copies, name, *after):
    (out,) = call(fold_kernel, name, (), (), [(copies, *parts.shape[1:])], [], 1, 2, (1,))(
        parts, *after
    )
    return out


def fold_kernel(parts, *refs):
    out = refs[-2]
    mine = parts[0]
    for at in range(1, parts.shape[0]):
        mine += parts[at]
    for at in range(out.shape[0]):
        out[at] = mine


def dft_table(width):
    index = np.arange(width)
    angle = 2.0 * np.pi * ((index[:, None] * index[None, :]) % width) / width
    cos, sin = np.cos(angle) / np.sqrt(width), -np.sin(angle) / np.sqrt(width)
    table = np.block([[cos, sin], [-sin, cos]]).astype(np.float32)
    lead = table.astype(jnp.bfloat16)
    trail = (table - lead.astype(np.float32)).astype(jnp.bfloat16)
    return np.concatenate([lead, lead, trail], axis=0)


def transform(re, im, table):
    rows = jnp.concatenate([re, im], axis=1)
    lead = rows.astype(BF16)
    trail = (rows - lead.astype(F32)).astype(BF16)
    out = jnp.dot(
        jnp.concatenate([lead, trail, lead], axis=1), table[...], preferred_element_type=F32
    )
    width = re.shape[1]
    return out[:, :width], out[:, width:]


def turn(parts):
    return jnp.concatenate([jnp.transpose(part) for part in parts], axis=0)


def add_slots(org, count, ext, acc, probe_re, probe_im, total, inten, table):
    width = probe_re.shape[0]
    bottom = ext.shape[2] - width
    lanes = lax.broadcasted_iota(jnp.int32, (width, width), 1)

    def split(value):
        return [value[i * width : (i + 1) * width] for i in range(GROUP)]

    def some(step, carry):
        slots = [step * GROUP + i for i in range(GROUP)]
        rows, blocks, cols, masks = [], [], [], []
        weights = []
        for slot in slots:
            col = lax.rem(org[1, slot], (ext.shape[1] - 1) * width)
            rows.append(lax.rem(org[0, slot], bottom))
            blocks.append(col // width)
            cols.append(lax.rem(col, width))
            masks.append(lanes >= cols[-1])
            weights.append((slot < count).astype(F32))
        obj, prb = [], []
        for i in range(GROUP):
            where = pl.ds(rows[i], width)
            obj.append(
                [
                    jnp.where(masks[i], ext[p, blocks[i], where, :], ext[p, blocks[i] + 1, where, :])
                    for p in range(2)
                ]
            )
            prb.append([pltpu.roll(part, cols[i], 1) for part in (probe_re, probe_im)])
        wave_re = [p[0] * o[0] - p[1] * o[1] for p, o in zip(prb, obj)]
        wave_im = [p[0] * o[1] + p[1] * o[0] for p, o in zip(prb, obj)]
        half_re, half_im = transform(
            jnp.concatenate(wave_re, axis=0), jnp.concatenate(wave_im, axis=0), table
        )
        far_re, far_im = transform(turn(split(half_re)), turn(split(half_im)), table)
        seen = jnp.concatenate([inten[slot] for slot in slots], axis=0)
        misfit = far_re * far_re + far_im * far_im - seen
        misfit = jnp.concatenate([m * w for m, w in zip(split(misfit), weights)], axis=0)
        half_im, half_re = transform(misfit * far_im, misfit * far_re, table)
        back_im, back_re = transform(turn(split(half_im)), turn(split(half_re)), table)
        back_re, back_im = split(back_re), split(back_im)
        sums = [jnp.zeros((width, width), F32)] * 2
        for i in range(GROUP):
            where = pl.ds(rows[i], width)
            grad = (
                prb[i][0] * back_re[i] + prb[i][1] * back_im[i],
                prb[i][0] * back_im[i] - prb[i][1] * back_re[i],
            )
            for p in range(2):
                acc[p, blocks[i], where, :] += jnp.where(masks[i], grad[p], 0.0)
                acc[p, blocks[i] + 1, where, :] += jnp.where(masks[i], 0.0, grad[p])
            own = (
                obj[i][0] * back_re[i] + obj[i][1] * back_im[i],
                obj[i][0] * back_im[i] - obj[i][1] * back_re[i],
            )
            home = lax.rem(width - cols[i], width)
            sums = [s + pltpu.roll(o, home, 1) for s, o in zip(sums, own)]
        for p in range(2):
            total[p] += sums[p]
        return carry

    lax.fori_loop(0, (count + GROUP - 1) // GROUP, some, 0)


def peak_of(probe_re, probe_im):
    power = probe_re * probe_re + probe_im * probe_im
    top = jnp.max(jnp.max(power, axis=0, keepdims=True), axis=1, keepdims=True)
    return step_object / (top + 1e-6)


class Copies:
    def __init__(self, sems):
        self.sems, self.used = sems, 0

    def start(self, *pairs):
        out = []
        for source, target in pairs:
            out.append(pltpu.make_async_copy(source, target, self.sems.at[self.used]))
            out[-1].start()
            self.used += 1
        return out


def wait(copies):
    for copy in copies:
        copy.wait()


def pack_kernel(tile, below, right, corner, sems):
    width = right.shape[2]
    wait(
        Copies(sems).start(
            (tile.at[:, :width, :], below),
            (tile.at[:, :, :width], right),
            (tile.at[:, :width, :width], corner),
        )
    )


def prepare_kernel(
    tile, probe_in, inten_in, table_in, ext, probe, inten, table, inten_out, raw, sems
):
    width = ext.shape[3]
    bottom = tile.shape[1]
    copies = Copies(sems)
    first = copies.start((inten_in, raw))
    rest = copies.start((probe_in, probe), (table_in, table))
    for j in range(ext.shape[1] - 1):
        rest += copies.start((tile.at[:, :, pl.ds(j * width, width)], ext.at[:, j, :bottom]))
    wait(first)
    for slot in range(raw.shape[0]):
        inten[slot] = jnp.transpose(raw[slot])
    wait(rest + copies.start((inten, inten_out)))


def first_kernel(
    org, counts, ext_in, below, right, corner, probe, inten, table,
    ext, acc_0, acc_1, acc_2, total, acc, sems,
):
    n = ext.shape[1] - 1
    width = ext.shape[3]
    bottom = ext.shape[2] - width
    for p in range(2):
        for j in range(n):
            ext[p, j, :bottom] = ext_in[p, j, :bottom]
            ext[p, j, bottom:] = below[p, :, j * width : (j + 1) * width]
        ext[p, n, :bottom] = right[p]
        ext[p, n, bottom:] = corner[p]
    acc[...] = jnp.zeros_like(acc)
    total[...] = jnp.zeros_like(total)
    add_slots(org, counts[0], ext, acc, probe[0], probe[1], total, inten, table)
    for p in range(2):
        for j, part in enumerate((acc_0, acc_1, acc_2)):
            part[p] = acc[p, j]


def strips_kernel(
    acc_0, acc_1, acc_2, from_left, from_right, after, own, up, down, sems
):
    del after, own
    width = up.shape[2]
    bottom = acc_0.shape[1] - width
    for p in range(2):
        for rows, block in ((slice(0, width), up), (slice(bottom, None), down)):
            block[p, 0] = acc_0[p, rows] + from_left[p, rows]
            block[p, 1] = acc_1[p, rows]
            block[p, 2] = acc_2[p, rows] + from_right[p, rows]


def own_kernel(ext, acc_0, acc_1, acc_2, probe, cur, sems):
    scale = peak_of(probe[0], probe[1])
    for p in range(2):
        for j, part in enumerate((acc_0, acc_1, acc_2)):
            cur[p, j] = ext[p, j] - scale * part[p]


def sides_kernel(old, from_left, from_right, probe, after, cur, sems):
    del after
    scale = peak_of(probe[0], probe[1])
    last = cur.shape[1] - 1
    for p in range(2):
        cur[p, 0] = old[p, 0] - scale * from_left[p]
        for j in range(1, last):
            cur[p, j] = old[p, j]
        cur[p, last] = old[p, last] - scale * from_right[p]


def rims_kernel(old, from_up, from_down, probe, after, cur, sems):
    del after
    scale = peak_of(probe[0], probe[1])
    width = cur.shape[3]
    bottom = cur.shape[2] - width
    for p in range(2):
        for j in range(cur.shape[1]):
            cur[p, j, :width] = old[p, j, :width] - scale * from_up[p, j]
            cur[p, j, width:bottom] = old[p, j, width:bottom]
            cur[p, j, bottom:] = old[p, j, bottom:] - scale * from_down[p, j]


def second_kernel(
    org, counts, cur, probe_in, gathered, share, inten_in, table_in,
    obj_out, side_out, probe_out, total_out, right_out, down_out, corner_out,
    acc, own, probe, total, inten, table, sems,
):
    n = cur.shape[1] - 1
    width = cur.shape[3]
    bottom = cur.shape[2] - width
    copies = Copies(sems)
    loads = copies.start((inten_in, inten), (table_in, table))
    for p in range(2):
        probe[p] = probe_in[p] - share[0] * gathered[p]
    acc[...] = jnp.zeros_like(acc)
    total[...] = jnp.zeros_like(total)
    wait(loads)
    add_slots(org, counts[0], cur, acc, probe[0], probe[1], total, inten, table)
    stores = copies.start((total, total_out), (probe, probe_out))
    scale = peak_of(probe[0], probe[1])
    for p in range(2):
        for j in range(n):
            own[p, j] = cur[p, j, :bottom] - scale * acc[p, j, :bottom]
            acc[p, j, bottom:] = scale * acc[p, j, bottom:]
        acc[p, n] = scale * acc[p, n]
    stores += copies.start(
        (acc.at[:, n, :bottom], right_out), (acc.at[:, n, bottom:], corner_out),
        (acc.at[:, :n, bottom:], down_out), (own.at[:, 0], side_out),
    )
    for j in range(1, n):
        cols = pl.ds(j * width, width)
        stores += copies.start((own.at[:, j], obj_out.at[:, :, cols]))
    wait(stores)


def final_kernel(
    obj_in, side_in, probe_in, from_left, from_up, from_corner, gathered, share,
    obj_out, probe_out, side, top, probe, sems,
):
    width = side.shape[2]
    copies = Copies(sems)
    places = [pl.ds((j + 1) * width, width) for j in range(top.shape[1])]
    loads = copies.start((side_in, side), (probe_in, probe))
    for j, cols in enumerate(places):
        loads += copies.start((obj_in.at[:, :width, cols], top.at[:, j]))
    wait(loads)
    for p in range(2):
        side[p] -= from_left[p]
        side[p, :width] -= from_up[p, 0] + from_corner[p]
        for j in range(top.shape[1]):
            top[p, j] -= from_up[p, j + 1]
        probe[p] -= share[0] * gathered[p]
    stores = copies.start((side, obj_out.at[:, :, :width]), (probe, probe_out))
    for j, cols in enumerate(places):
        stores += copies.start((top.at[:, j], obj_out.at[:, :width, cols]))
    wait(stores)


def call(kernel, name, smem, far, outs, scratch, copies, mib, unread=(), **more):
    kinds = {True: pltpu.HBM, False: pltpu.VMEM}

    def run(*operands):
        where = [pltpu.SMEM if at in smem else kinds[at in far] for at in range(len(operands))]
        held = [kinds[-1 - at in far] for at in range(len(outs))]
        where = [pl.ANY if at in unread else space for at, space in enumerate(where)]
        operands = [
            value if space in (pltpu.SMEM, pl.ANY) else pltpu.with_memory_space_constraint(value, space)
            for value, space in zip(operands, where)
        ]
        return pl.pallas_call(
            kernel,
            out_shape=[space(s, F32) if isinstance(s, tuple) else space(s.shape, s.dtype) for s, space in zip(outs, held)],
            in_specs=[pl.BlockSpec(memory_space=space) for space in where],
            out_specs=[pl.BlockSpec(memory_space=space) for space in held],
            scratch_shapes=[
                *(pltpu.VMEM(s, F32) if isinstance(s, tuple) else pltpu.VMEM(s.shape, s.dtype) for s in scratch),
                pltpu.SemaphoreType.DMA((copies,)),
            ],
            compiler_params=pltpu.CompilerParams(vmem_limit_bytes=mib * 1024 * 1024),
            name=name,
            **more,
        )(*operands)

    return run


def body(object_planes, probe, anchors, counts, intensity):
    rows, cols = object_planes.shape[1:]
    w = probe.shape[1]
    org = anchors[0, 0].T
    count = counts[0]
    inten = intensity[0, 0]
    table = jnp.asarray(dft_table(w))
    kept = jax.ShapeDtypeStruct(table.shape, table.dtype)
    slots = inten.shape
    n = cols // w
    tall, square = (2, rows + w, w), (2, w, w)
    blocks, strip = (2, n + 1, rows + w, w), (2, n + 1, w, w)
    share = jnp.full((1,), step_probe / (lax.axis_size("tx") * lax.axis_size("ty")), F32)

    below, right, corner = call(
        pack_kernel, "pack", (), (0,), [(2, w, cols), (2, rows, w), square], [], 3, 2
    )(object_planes)
    right, below, corner = shift(right, 0, -1), shift(below, -1, 0), shift(corner, -1, -1)
    ext, start, inten_near, table_near, inten = call(
        prepare_kernel, "prepare", (), (0, 1, 2, 3, -5),
        [blocks, square, slots, kept, slots], [slots], 6, 4,
    )(object_planes, probe, inten, table)
    ext, acc_0, acc_1, acc_2, total = call(
        first_kernel, "first_pass", (0, 1), (), [blocks, tall, tall, tall, square], [blocks], 1, 8
    )(org, count, ext, below, right, corner, start, inten_near, table_near)
    from_left, from_right = shift(acc_2, 0, 1), shift(acc_0, 0, -1)
    hint = pl.CostEstimate(flops=1 << 20, bytes_accessed=1 << 23, transcendentals=0)
    (cur,) = call(own_kernel, "own_step", (), (), [blocks], [], 1, 8, cost_estimate=hint)(
        ext, acc_0, acc_1, acc_2, start
    )
    parts = sum_in_plane(total)
    up, down = call(strips_kernel, "strips", (), (), [strip, strip], [], 1, 6, (5, 6))(
        acc_0, acc_1, acc_2, from_left, from_right, parts, cur
    )
    from_up, from_down = shift(down, 1, 0), shift(up, -1, 0)
    (cur,) = call(sides_kernel, "sides_step", (), (), [blocks], [], 1, 8, (4,), cost_estimate=hint)(
        cur, from_left, from_right, start, parts
    )
    parts = sum_along(parts, cur)
    (cur,) = call(rims_kernel, "rims_step", (), (), [blocks], [], 1, 8, (4,), cost_estimate=hint)(
        cur, from_up, from_down, start, parts
    )
    gathered = collect(parts)
    obj, side, current, total, to_right, to_down, to_corner = call(
        second_kernel, "second_pass", (0, 1, 5), (6, 7, *range(-7, 0)),
        [(2, rows, cols), (2, rows, w), square, square, (2, rows, w), (2, n, w, w), square],
        [blocks, (2, n, rows, w), square, square, slots, kept], n + 7, 10,
    )(org, count, cur, start, gathered, share, inten, table)
    from_left, from_up = shift(to_right, 0, 1), shift(to_down, 1, 0)
    from_corner = shift(to_corner, 1, 1)
    gathered = collect(sum_along(sum_in_plane(total)))
    obj, current = call(
        final_kernel, "finish", (7,), (0, 1, 2, -1, -2), [(2, rows, cols), square],
        [(2, rows, w), (2, n - 1, w, w), square], 2 * n + 2, 3, input_output_aliases={0: 0},
    )(obj, side, current, from_left, from_up, from_corner, gathered, share)
    return obj, current


def solution(mesh):
    return jax.shard_map(
        body,
        mesh=mesh,
        in_specs=(
            P(None, "ty", "tx"),
            P(),
            P("ty", "tx", None, None),
            P("ty", "tx"),
            P("ty", "tx", None, None, None),
        ),
        out_specs=(P(None, "ty", "tx"), P()),
        check_vma=False,
    )
```

```python
import jax
import jax.numpy as jnp
import numpy as np
from jax import lax
from jax.experimental import pallas as pl
from jax.experimental.pallas import tpu as pltpu
from jax.sharding import PartitionSpec as P

step_object = 1.0
step_probe = 1.0
GROUP = 4
CORES = 2
F32 = jnp.float32
BF16 = jnp.bfloat16


def shift(value, rows, cols):
    n_r, n_c = lax.axis_size("ty"), lax.axis_size("tx")
    if cols == 0:
        return lax.ppermute(
            value, "ty", [(a, a + rows) for a in range(n_r) if 0 <= a + rows < n_r]
        )
    if rows == 0:
        return lax.ppermute(
            value, "tx", [(b, b + cols) for b in range(n_c) if 0 <= b + cols < n_c]
        )
    pairs = [
        (b * n_r + a, (b + cols) * n_r + a + rows)
        for a in range(n_r)
        for b in range(n_c)
        if 0 <= a + rows < n_r and 0 <= b + cols < n_c
    ]
    return lax.ppermute(value, ("tx", "ty"), pairs)


def swap(parts, axes, groups):
    return lax.all_to_all(parts, axes, 0, 0, axis_index_groups=groups, tiled=True)


def device_groups():
    n_r, n_c = lax.axis_size("ty"), lax.axis_size("tx")
    depth = n_c // CORES
    plane = [
        [(z * CORES + c) * n_r + a for c in range(CORES) for a in range(n_r)] for z in range(depth)
    ]
    return plane, [[z * CORES + c for z in range(depth)] for c in range(CORES)]


def sum_in_plane(value):
    plane, line = device_groups()
    parts = value.reshape(len(plane[0]), -1, value.shape[-1])
    return fold(swap(parts, ("tx", "ty"), plane), len(line[0]), "fold_plane")


def sum_along(parts):
    plane, line = device_groups()
    parts = fold(swap(parts, "tx", line), len(plane[0]), "fold_line")
    parts = swap(parts, ("tx", "ty"), plane)
    return parts.reshape(2, -1, parts.shape[-1])


def fold(parts, copies, name):
    (out,) = call(fold_kernel, name, (), (), [(copies, *parts.shape[1:])], [], 1, 1)(parts)
    return out


def fold_kernel(parts, out, sems):
    mine = parts[0]
    for at in range(1, parts.shape[0]):
        mine += parts[at]
    for at in range(out.shape[0]):
        out[at] = mine


def dft_table(width):
    index = np.arange(width)
    angle = 2.0 * np.pi * ((index[:, None] * index[None, :]) % width) / width
    cos, sin = np.cos(angle) / np.sqrt(width), -np.sin(angle) / np.sqrt(width)
    table = np.block([[cos, sin], [-sin, cos]]).astype(np.float32)
    lead = table.astype(jnp.bfloat16)
    trail = (table - lead.astype(np.float32)).astype(jnp.bfloat16)
    return np.concatenate([lead, lead, trail], axis=0)


def transform(re, im, table):
    rows = jnp.concatenate([re, im], axis=1)
    lead = rows.astype(BF16)
    trail = (rows - lead.astype(F32)).astype(BF16)
    out = jnp.dot(
        jnp.concatenate([lead, trail, lead], axis=1), table[...], preferred_element_type=F32
    )
    width = re.shape[1]
    return out[:, :width], out[:, width:]


def turn(parts):
    return jnp.concatenate([jnp.transpose(part) for part in parts], axis=0)


def add_slots(org, count, ext, acc, probe_re, probe_im, total, inten, table):
    width = probe_re.shape[0]
    bottom = ext.shape[2] - width
    lanes = lax.broadcasted_iota(jnp.int32, (width, width), 1)

    def split(value):
        return [value[i * width : (i + 1) * width] for i in range(GROUP)]

    def some(step, carry):
        slots = [step * GROUP + i for i in range(GROUP)]
        rows, blocks, cols, masks = [], [], [], []
        weights = []
        for slot in slots:
            col = lax.rem(org[1, slot], (ext.shape[1] - 1) * width)
            rows.append(lax.rem(org[0, slot], bottom))
            blocks.append(col // width)
            cols.append(lax.rem(col, width))
            masks.append(lanes >= cols[-1])
            weights.append((slot < count).astype(F32))
        obj, prb = [], []
        for i in range(GROUP):
            where = pl.ds(rows[i], width)
            obj.append(
                [
                    jnp.where(masks[i], ext[p, blocks[i], where, :], ext[p, blocks[i] + 1, where, :])
                    for p in range(2)
                ]
            )
            prb.append([pltpu.roll(part, cols[i], 1) for part in (probe_re, probe_im)])
        wave_re = [p[0] * o[0] - p[1] * o[1] for p, o in zip(prb, obj)]
        wave_im = [p[0] * o[1] + p[1] * o[0] for p, o in zip(prb, obj)]
        half_re, half_im = transform(
            jnp.concatenate(wave_re, axis=0), jnp.concatenate(wave_im, axis=0), table
        )
        far_re, far_im = transform(turn(split(half_re)), turn(split(half_im)), table)
        seen = jnp.concatenate([inten[slot] for slot in slots], axis=0)
        misfit = far_re * far_re + far_im * far_im - seen
        misfit = jnp.concatenate([m * w for m, w in zip(split(misfit), weights)], axis=0)
        half_im, half_re = transform(misfit * far_im, misfit * far_re, table)
        back_im, back_re = transform(turn(split(half_im)), turn(split(half_re)), table)
        back_re, back_im = split(back_re), split(back_im)
        sums = [jnp.zeros((width, width), F32)] * 2
        for i in range(GROUP):
            where = pl.ds(rows[i], width)
            grad = (
                prb[i][0] * back_re[i] + prb[i][1] * back_im[i],
                prb[i][0] * back_im[i] - prb[i][1] * back_re[i],
            )
            for p in range(2):
                acc[p, blocks[i], where, :] += jnp.where(masks[i], grad[p], 0.0)
                acc[p, blocks[i] + 1, where, :] += jnp.where(masks[i], 0.0, grad[p])
            own = (
                obj[i][0] * back_re[i] + obj[i][1] * back_im[i],
                obj[i][0] * back_im[i] - obj[i][1] * back_re[i],
            )
            home = lax.rem(width - cols[i], width)
            sums = [s + pltpu.roll(o, home, 1) for s, o in zip(sums, own)]
        for p in range(2):
            total[p] += sums[p]
        return carry

    lax.fori_loop(0, (count + GROUP - 1) // GROUP, some, 0)


def peak_of(probe_re, probe_im):
    power = probe_re * probe_re + probe_im * probe_im
    top = jnp.max(jnp.max(power, axis=0, keepdims=True), axis=1, keepdims=True)
    return step_object / (top + 1e-6)


class Copies:
    def __init__(self, sems):
        self.sems, self.used = sems, 0

    def start(self, *pairs):
        out = []
        for source, target in pairs:
            out.append(pltpu.make_async_copy(source, target, self.sems.at[self.used]))
            out[-1].start()
            self.used += 1
        return out


def wait(copies):
    for copy in copies:
        copy.wait()


def pack_kernel(tile, below, right, corner, sems):
    width = right.shape[2]
    wait(
        Copies(sems).start(
            (tile.at[:, :width, :], below),
            (tile.at[:, :, :width], right),
            (tile.at[:, :width, :width], corner),
        )
    )


def prepare_kernel(
    tile, probe_in, inten_in, table_in, ext, probe, inten, table, inten_out, raw, sems
):
    width = ext.shape[3]
    bottom = tile.shape[1]
    copies = Copies(sems)
    first = copies.start((inten_in, raw))
    rest = copies.start((probe_in, probe), (table_in, table))
    for j in range(ext.shape[1] - 1):
        rest += copies.start((tile.at[:, :, pl.ds(j * width, width)], ext.at[:, j, :bottom]))
    wait(first)
    for slot in range(raw.shape[0]):
        inten[slot] = jnp.transpose(raw[slot])
    wait(rest + copies.start((inten, inten_out)))


def first_kernel(
    org, counts, ext_in, below, right, corner, probe, inten, table,
    ext, acc_0, acc_1, acc_2, total, acc, sems,
):
    n = ext.shape[1] - 1
    width = ext.shape[3]
    bottom = ext.shape[2] - width
    for p in range(2):
        for j in range(n):
            ext[p, j, :bottom] = ext_in[p, j, :bottom]
            ext[p, j, bottom:] = below[p, :, j * width : (j + 1) * width]
        ext[p, n, :bottom] = right[p]
        ext[p, n, bottom:] = corner[p]
    acc[...] = jnp.zeros_like(acc)
    total[...] = jnp.zeros_like(total)
    add_slots(org, counts[0], ext, acc, probe[0], probe[1], total, inten, table)
    for p in range(2):
        for j, part in enumerate((acc_0, acc_1, acc_2)):
            part[p] = acc[p, j]


def strips_kernel(acc_0, acc_1, acc_2, from_left, from_right, after, up, down, sems):
    del after
    width = up.shape[2]
    bottom = acc_0.shape[1] - width
    for p in range(2):
        for rows, block in ((slice(0, width), up), (slice(bottom, None), down)):
            block[p, 0] = acc_0[p, rows] + from_left[p, rows]
            block[p, 1] = acc_1[p, rows]
            block[p, 2] = acc_2[p, rows] + from_right[p, rows]


def second_kernel(
    org, counts, ext, acc_0, acc_1, acc_2, from_left, from_right, from_up, from_down,
    probe_in, gathered, share, inten_in, table_in,
    obj_out, side_out, probe_out, total_out, right_out, down_out, corner_out,
    cur, acc, own, probe, total, inten, table, sems,
):
    n = cur.shape[1] - 1
    width = cur.shape[3]
    bottom = cur.shape[2] - width
    copies = Copies(sems)
    loads = copies.start((inten_in, inten), (table_in, table))
    scale = peak_of(probe_in[0], probe_in[1])
    mid = slice(width, bottom)
    for p in range(2):
        probe[p] = probe_in[p] - share[0] * gathered[p]
        rows = ((slice(0, width), from_up), (mid, None), (slice(bottom, None), from_down))
        for j, (part, side) in enumerate(
            ((acc_0, from_left), (acc_1, None), (acc_2, from_right))
        ):
            for where, edge in rows:
                value = part[p, where]
                if side is not None:
                    value += side[p, where]
                if edge is not None:
                    value += edge[p, j]
                cur[p, j, where] = ext[p, j, where] - scale * value
    acc[...] = jnp.zeros_like(acc)
    total[...] = jnp.zeros_like(total)
    wait(loads)
    add_slots(org, counts[0], cur, acc, probe[0], probe[1], total, inten, table)
    stores = copies.start((total, total_out), (probe, probe_out))
    scale = peak_of(probe[0], probe[1])
    for p in range(2):
        for j in range(n):
            own[p, j] = cur[p, j, :bottom] - scale * acc[p, j, :bottom]
            acc[p, j, bottom:] = scale * acc[p, j, bottom:]
        acc[p, n] = scale * acc[p, n]
    stores += copies.start(
        (acc.at[:, n, :bottom], right_out), (acc.at[:, n, bottom:], corner_out),
        (acc.at[:, :n, bottom:], down_out), (own.at[:, 0], side_out),
    )
    for j in range(1, n):
        cols = pl.ds(j * width, width)
        stores += copies.start((own.at[:, j], obj_out.at[:, :, cols]))
    wait(stores)


def final_kernel(
    obj_in, side_in, probe_in, from_left, from_up, from_corner, gathered, share,
    obj_out, probe_out, side, top, probe, sems,
):
    width = side.shape[2]
    copies = Copies(sems)
    places = [pl.ds((j + 1) * width, width) for j in range(top.shape[1])]
    loads = copies.start((side_in, side), (probe_in, probe))
    for j, cols in enumerate(places):
        loads += copies.start((obj_in.at[:, :width, cols], top.at[:, j]))
    wait(loads)
    for p in range(2):
        side[p] -= from_left[p]
        side[p, :width] -= from_up[p, 0] + from_corner[p]
        for j in range(top.shape[1]):
            top[p, j] -= from_up[p, j + 1]
        probe[p] -= share[0] * gathered[p]
    stores = copies.start((side, obj_out.at[:, :, :width]), (probe, probe_out))
    for j, cols in enumerate(places):
        stores += copies.start((top.at[:, j], obj_out.at[:, :width, cols]))
    wait(stores)


def call(kernel, name, smem, far, outs, scratch, copies, mib, **more):
    kinds = {True: pltpu.HBM, False: pltpu.VMEM}

    def run(*operands):
        where = [pltpu.SMEM if at in smem else kinds[at in far] for at in range(len(operands))]
        held = [kinds[-1 - at in far] for at in range(len(outs))]
        operands = [
            value if space is pltpu.SMEM else pltpu.with_memory_space_constraint(value, space)
            for value, space in zip(operands, where)
        ]
        return pl.pallas_call(
            kernel,
            out_shape=[space(s, F32) if isinstance(s, tuple) else space(s.shape, s.dtype) for s, space in zip(outs, held)],
            in_specs=[pl.BlockSpec(memory_space=space) for space in where],
            out_specs=[pl.BlockSpec(memory_space=space) for space in held],
            scratch_shapes=[
                *(pltpu.VMEM(s, F32) if isinstance(s, tuple) else pltpu.VMEM(s.shape, s.dtype) for s in scratch),
                pltpu.SemaphoreType.DMA((copies,)),
            ],
            compiler_params=pltpu.CompilerParams(vmem_limit_bytes=mib * 1024 * 1024),
            name=name,
            **more,
        )(*operands)

    return run


def body(object_planes, probe, anchors, counts, intensity):
    rows, cols = object_planes.shape[1:]
    w = probe.shape[1]
    org = anchors[0, 0].T
    count = counts[0]
    inten = intensity[0, 0]
    table = jnp.asarray(dft_table(w))
    kept = jax.ShapeDtypeStruct(table.shape, table.dtype)
    slots = inten.shape
    n = cols // w
    tall, square = (2, rows + w, w), (2, w, w)
    blocks, strip = (2, n + 1, rows + w, w), (2, n + 1, w, w)
    share = jnp.full((1,), step_probe / (lax.axis_size("tx") * lax.axis_size("ty")), F32)

    below, right, corner = call(
        pack_kernel, "pack", (), (0,), [(2, w, cols), (2, rows, w), square], [], 3, 2
    )(object_planes)
    right, below, corner = shift(right, 0, -1), shift(below, -1, 0), shift(corner, -1, -1)
    ext, start, inten_near, table_near, inten = call(
        prepare_kernel, "prepare", (), (0, 1, 2, 3, -5),
        [blocks, square, slots, kept, slots], [slots], 6, 4,
    )(object_planes, probe, inten, table)
    ext, acc_0, acc_1, acc_2, total = call(
        first_kernel, "first_pass", (0, 1), (), [blocks, tall, tall, tall, square], [blocks], 1, 8
    )(org, count, ext, below, right, corner, start, inten_near, table_near)
    from_left, from_right = shift(acc_2, 0, 1), shift(acc_0, 0, -1)
    parts = sum_in_plane(total)
    up, down = call(strips_kernel, "strips", (), (), [strip, strip], [], 1, 1)(
        acc_0, acc_1, acc_2, from_left, from_right, parts
    )
    from_up, from_down = shift(down, 1, 0), shift(up, -1, 0)
    gathered = sum_along(parts)
    obj, side, current, total, to_right, to_down, to_corner = call(
        second_kernel, "second_pass", (0, 1, 12), (13, 14, *range(-7, 0)),
        [(2, rows, cols), (2, rows, w), square, square, (2, rows, w), (2, n, w, w), square],
        [blocks, blocks, (2, n, rows, w), square, square, slots, kept], n + 7, 11,
    )(
        org, count, ext, acc_0, acc_1, acc_2, from_left, from_right, from_up, from_down,
        start, gathered, share, inten, table,
    )
    from_left, from_up = shift(to_right, 0, 1), shift(to_down, 1, 0)
    from_corner = shift(to_corner, 1, 1)
    gathered = sum_along(sum_in_plane(total))
    obj, current = call(
        final_kernel, "finish", (7,), (0, 1, 2, -1, -2), [(2, rows, cols), square],
        [(2, rows, w), (2, n - 1, w, w), square], 2 * n + 2, 3, input_output_aliases={0: 0},
    )(obj, side, current, from_left, from_up, from_corner, gathered, share)
    return obj, current


def solution(mesh):
    return jax.shard_map(
        body,
        mesh=mesh,
        in_specs=(
            P(None, "ty", "tx"),
            P(),
            P("ty", "tx", None, None),
            P("ty", "tx"),
            P("ty", "tx", None, None, None),
        ),
        out_specs=(P(None, "ty", "tx"), P()),
        check_vma=False,
    )
```
